256 devices in a mesh: tile: 128 (over y, x, z), chol: 2 (over core).
Axes of the slice: x: 4, y: 4, z: 8, core: 2. Of those that a mesh axis runs over, the one named last changes fastest.
Arguments:
- amplitudes: bfloat16 [120, 2, 1024, 1024], P('chol', None, 'tile'), may hold values from -6 to 6
- cholesky: bfloat16 [120, 1024, 896], P(None, 'tile', 'chol'), may hold values from -0.0625 to 0.0625
Outputs:
- cycle_term: bfloat16 [120, 2, 1024, 1024], P('chol', None, 'tile')
The draws below stay inside these ranges and needn't reach their ends.
All inputs are finite; a program needn't handle non-finite values.
Results may differ from the reference program's by a relative error of at most 0.0049.
Values may be sent and summed in bfloat16 or wider, within the bound.
A program may use at most 64 MiB of HBM per device.

```python
import jax
import jax.numpy as jnp
from jax import lax

O = 120
V = 1024
NCHOL = 896
JS = 2


def level_of(stream_key, dims, shards, least, largest):
    loudness, own = 1.0, jax.random.fold_in(stream_key, 6)
    for dim, parts in shards:
        heights = jnp.exp(jax.random.uniform(jax.random.fold_in(own, dim), (parts,), jnp.float32, least / len(shards), largest / len(shards)))
        loudness = loudness * jnp.repeat(heights, dims[dim] // parts).reshape([-1 if axis == dim else 1 for axis in range(len(dims))])
    return loudness


def gaussian(stream_key, extent, spread, bound, split=(), held_as=jnp.bfloat16):
    drawn = jax.random.normal(stream_key, extent, jnp.float32) * spread
    if len(split) > 0:
        drawn = level_of(stream_key, extent, split, -0.22, 0.18) * drawn
    return jnp.clip(drawn, min=-bound, max=bound).astype(held_as)


def setup_inputs(seed: int = 0) -> dict:
    key_list = jax.random.split(jax.random.key(seed), 3)
    amplitudes = gaussian(key_list[0], (O, JS, V, V), 1.0, 6.0, ((0, 2), (2, 128)))
    cholesky = gaussian(key_list[1], (O, V, NCHOL), ((O * V * NCHOL) ** 0.5) ** -0.5, 0.0625, ((1, 128), (2, 2)))
    return dict(amplitudes=amplitudes, cholesky=cholesky)


def reference(amplitudes, cholesky):
    def add_orbital(running_sum, pair):
        amp_block, vectors = pair
        flat_block = amp_block.reshape(JS * V, V)
        return running_sum + jnp.dot(flat_block, vectors, preferred_element_type=jnp.float32), None

    running_sum, unused = lax.scan(add_orbital, jnp.zeros((JS * V, NCHOL), jnp.float32), (amplitudes, cholesky))
    intermediate = running_sum.astype(jnp.bfloat16)

    def one_row(vectors):
        product = jnp.dot(intermediate, vectors.T, preferred_element_type=jnp.float32)
        return product.astype(jnp.bfloat16).reshape(JS, V, V)

    return lax.map(one_row, cholesky)
```

```python
import functools

import jax
import jax.numpy as jnp
from jax import lax
from jax.experimental import pallas as pl
from jax.experimental.pallas import tpu as pltpu
from jax.sharding import PartitionSpec as P

MESH = pl.DeviceIdType.MESH
BF, F32 = jnp.bfloat16, jnp.float32
TILES, CORES, K, A, VEC = 128, 2, 60, 8, 448
ALLVEC = CORES * VEC
GRP = 16
LANES = 512
HALF = TILES // CORES


def barrel(blocks):
    u = lax.broadcasted_iota(jnp.int32, blocks[0].shape, 1) // A
    for bit in (1, 2, 4, 8):
        take = (u & bit) != 0
        blocks = [jnp.where(take, blocks[(i + bit) % GRP], blocks[i]) for i in range(GRP)]
    return blocks


def kernel(t_ref, l_ref, recv2, send1, recv1, lp, lrot, part, rs1, rb1, acc2, rs2, rb2, acc3, rs3, rb3, inter, send2,
           ssem1, rsem1, lsem, rsems, agsems, ssem2, rsem2):
    me, core = lax.axis_index("tile"), lax.axis_index("chol")
    y, x, z = me // 32, lax.rem(me // 8, 4), lax.rem(me, 8)
    c_a, c_b = jnp.where(core == 0, x, y), jnp.where(core == 0, y, x)
    spin = lax.rem(me, GRP)
    own_core = lax.rem(me, CORES)
    slot = me // CORES

    def tile_at(a, b, zz):
        return jnp.where(core == 0, b * 32 + a * 8, a * 32 + b * 8) + zz

    def remote(src, dst, send_sem, recv_sem, tile, to_core=core):
        return pltpu.make_async_remote_copy(src_ref=src, dst_ref=dst, send_sem=send_sem, recv_sem=recv_sem,
                                            device_id=(tile, to_core), device_id_type=MESH)

    def shuffle(j):
        def lane_tile(m, _):
            lanes = pl.ds(pl.multiple_of(m * 128, 128), 128)
            for q in range(4):
                blocks = []
                for i in range(GRP):
                    if q * GRP + i < K:
                        block = t_ref[q * GRP + i, j, :, lanes].astype(F32)
                        blocks.append(pltpu.roll(block, A * i, 1) if i else block)
                    else:
                        blocks.append(jnp.zeros((A, 128), F32))
                blocks = barrel(blocks)
                for g in range(GRP):
                    send1[j, m * GRP + g, :, q * 128:(q + 1) * 128] = blocks[-g % GRP].astype(BF)
            return 0
        lax.fori_loop(0, TILES // GRP, lane_tile, 0)

    def start1(j, lo, hi):
        def one(q, _):
            tile = lax.rem(y + q // 32, 4) * 32 + lax.rem(x + lax.rem(q // 8, 4), 4) * 8 + lax.rem(z + lax.rem(q, 8), 8)
            src, dst = send1.at[j, tile], recv1.at[j, core, slot]
            stays = jnp.logical_and(tile == me, own_core == core)

            @pl.when(stays)
            def _():
                pltpu.make_async_copy(src, dst, rsem1.at[j]).start()

            @pl.when(jnp.logical_not(stays))
            def _():
                remote(src, dst, ssem1.at[j], rsem1.at[j], tile, own_core).start()
            return 0
        lax.fori_loop(lo, hi, one, 0)

    def start2(j, lo, hi):
        def one(q, _):
            tile = (lax.rem(y + q // 16, 4) * 32 + lax.rem(x + lax.rem(q // 4, 4), 4) * 8
                    + 2 * lax.rem(z // 2 + lax.rem(q, 4), 4) + core)
            for to_core in range(CORES):
                src, dst = send2.at[j, to_core, tile // 2], recv2.at[j, me]
                stays = jnp.logical_and(tile == me, to_core == core)

                @pl.when(stays)
                def _():
                    pltpu.make_async_copy(src, dst, rsem2.at[j]).start()

                @pl.when(jnp.logical_not(stays))
                def _():
                    remote(src, dst, ssem2.at[j], rsem2.at[j], tile, to_core).start()
            return 0
        lax.fori_loop(lo, hi, one, 0)

    def wait_bytes(ref, sem):
        pltpu.make_async_copy(ref, ref, sem).wait()

    def vectors():
        row = lax.broadcasted_iota(jnp.int32, (VEC, LANES), 0)
        column = lax.broadcasted_iota(jnp.int32, (VEC, LANES), 1)
        move = (column == row + (LANES - VEC) * core).astype(BF)
        for n in range(0, 120, 40):
            wide = jnp.dot(l_ref[n:n + 40].reshape(40 * A, VEC), move, preferred_element_type=F32)
            lp[core, n:n + 40] = wide.astype(BF).reshape(40, A, LANES)
        to_sibling = remote(lp.at[core], lp.at[core], lsem.at[0], lsem.at[1], me, 1 - core)
        to_sibling.start()
        return to_sibling

    def turn_vectors():
        def one(n, _):
            half, u = n // 64, lax.rem(n, 64)
            k = (u // GRP) * GRP + lax.rem(lax.rem(u, GRP) + GRP - spin, GRP)
            row = half * K + jnp.minimum(k, K - 1)
            left, right = lp[0, row].astype(F32), lp[1, row].astype(F32)
            whole = jnp.concatenate([left[:, :384], left[:, 384:] + right[:, :128], right[:, 128:]], axis=1)
            lrot[half, u] = jnp.where(k < K, whole, 0.0).astype(BF)
            return 0
        lax.fori_loop(0, 128, one, 0)

    def multiply1(j):
        for lo, hi in ((0, 256), (256, 512), (512, 768), (768, 896)):
            total = None
            for half in range(CORES):
                term = jnp.dot(recv1[j, half].reshape(HALF * A, LANES), lrot[half, :, :, lo:hi].reshape(LANES, hi - lo),
                               preferred_element_type=F32)
                total = term if total is None else total + term
            total = total.reshape(HALF, A, hi - lo)
            part[:, :, lo:hi] = total
            rs1[j, :, :, lo:hi] = total.astype(BF)

    def add_up(j, fill):
        copies = []

        def go(copy):
            copy.start()
            copies.append(copy)

        def arrive(first):
            for copy in copies[first:]:
                copy.wait_recv()

        for d in range(1, 4):
            a = lax.rem(c_a + d, 4)
            go(remote(rs1.at[j, pl.ds(a * 16, 16)], rb1.at[j, d - 1], rsems.at[j, 0, d - 1], rsems.at[j, 1, d - 1],
                      tile_at(a, c_b, z)))
        fill()
        arrive(0)

        def first(n, _):
            total = part[c_a * 16 + n]
            for d in range(3):
                total = total + rb1[j, d, n].astype(F32)
            acc2[n] = total
            rs2[j, n] = total.astype(BF)
            return 0
        lax.fori_loop(0, 16, first, 0)
        for d in range(1, 4):
            b = lax.rem(c_b + d, 4)
            go(remote(rs2.at[j, pl.ds(b * 4, 4)], rb2.at[j, d - 1], rsems.at[j, 0, 2 + d], rsems.at[j, 1, 2 + d],
                      tile_at(c_a, b, z)))
        fill()
        arrive(3)

        def second(n, _):
            total = acc2[c_b * 4 + n]
            for d in range(3):
                total = total + rb2[j, d, n].astype(F32)
            acc3[n] = total
            rs3[j, n] = total.astype(BF)
            return 0
        lax.fori_loop(0, 4, second, 0)
        for d in range(1, 8):
            zz = lax.rem(z + d, 8)
            go(remote(rs3.at[j, lax.rem(zz, 4)], rb3.at[j, d - 1], rsems.at[j, 0, 5 + d], rsems.at[j, 1, 5 + d],
                      tile_at(c_a, c_b, zz)))
        fill()
        arrive(6)
        total = acc3[lax.rem(z, 4)]
        for d in range(7):
            total = total + rb3[j, d].astype(F32)
        mine = c_a * 16 + c_b * 4 + lax.rem(z, 4)
        inter[j, mine] = total.astype(BF)

        def share(first, count, n, tile, source):
            src = inter.at[j, pl.ds(first, count)]
            go(remote(src, src, agsems.at[j, 0, n], agsems.at[j, 1, n], tile))
            landed.append(remote(src, inter.at[j, pl.ds(source, count)], agsems.at[j, 0, n], agsems.at[j, 1, n], tile))

        landed = []
        base = c_a * 16 + c_b * 4
        for n, d in enumerate((1, 7, 2)):
            share(mine, 1, n, tile_at(c_a, c_b, lax.rem(z + d, 8)), base + lax.rem(z + 8 - d, 4))
        fill()
        for copy in landed:
            copy.wait_recv()
        landed.clear()
        for d in range(1, 4):
            share(base, 4, 2 + d, tile_at(c_a, lax.rem(c_b + d, 4), z), c_a * 16 + lax.rem(c_b + 4 - d, 4) * 4)
        fill()
        for copy in landed:
            copy.wait_recv()
        landed.clear()
        for d in range(1, 4):
            share(c_a * 16, 16, 5 + d, tile_at(lax.rem(c_a + d, 4), c_b, z), lax.rem(c_a + 4 - d, 4) * 16)
        fill()
        for copy in landed:
            copy.wait_recv()
        return copies

    def multiply2(j):
        for half in range(CORES):
            for lo in (0, 256):
                block = lax.dot_general(inter[j].reshape(HALF * A, ALLVEC),
                                        lrot[half, lo // A:(lo + 256) // A].reshape(256, ALLVEC),
                                        (((1,), (1,)), ((), ())), preferred_element_type=F32)
                send2[j, half, :, :, lo:lo + 256] = block.astype(BF).reshape(HALF, A, 256)

    class Filler:
        def __init__(self, begin, cuts):
            self.begin, self.cuts = begin, cuts

        def __call__(self):
            lo = self.cuts.pop(0)
            self.begin(lo, self.cuts[0])

    shuffle(0)
    start1(0, 0, TILES)
    to_sibling = vectors()
    shuffle(1)
    to_sibling.wait_recv()
    turn_vectors()
    fill1 = Filler(lambda lo, hi: start1(1, lo, hi), [0, 32, 52, 68, 84, 100, 116, 128])
    fill1()
    wait_bytes(recv1.at[0], rsem1.at[0])
    multiply1(0)
    copies = add_up(0, fill1)
    multiply2(0)
    fill2 = Filler(lambda lo, hi: start2(0, lo, hi), [0, 16, 26, 34, 42, 50, 58, 64])
    fill2()
    wait_bytes(recv1.at[1], rsem1.at[1])
    multiply1(1)
    copies += add_up(1, fill2)
    multiply2(1)
    start2(1, 0, HALF)
    for j in range(2):
        wait_bytes(recv2.at[j], rsem2.at[j])
    for copy in copies + [to_sibling]:
        copy.wait_send()
    for j in range(2):
        @pl.when(own_core == core)
        def _():
            wait_bytes(send1.at[j, pl.ds(0, TILES - 1)], ssem1.at[j])
            wait_bytes(recv2.at[j, pl.ds(0, TILES - 1)], ssem2.at[j])

        @pl.when(own_core != core)
        def _():
            wait_bytes(send1.at[j], ssem1.at[j])
            wait_bytes(recv2.at[j], ssem2.at[j])


def unshuffle(r_ref, o_ref):
    for j in range(2):
        for q in range(4):
            blocks = [r_ref[j, g, :, q * 128:(q + 1) * 128].astype(F32) for g in range(GRP)]
            blocks = barrel(blocks)
            for i in range(min(GRP, K - q * GRP)):
                block = blocks[-i % GRP]
                o_ref[q * GRP + i, j] = (pltpu.roll(block, 128 - A * i, 1) if i else block).astype(BF)


def shards(amplitudes, cholesky):
    vmem = pl.BlockSpec(memory_space=pltpu.VMEM)
    dma, V = pltpu.SemaphoreType.DMA, pltpu.VMEM
    landed = pl.pallas_call(
        kernel,
        out_shape=jax.ShapeDtypeStruct((2, TILES, A, LANES), BF),
        in_specs=[vmem, vmem],
        out_specs=pl.BlockSpec(memory_space=pl.ANY),
        scratch_shapes=[
            V((2, TILES, A, LANES), BF), V((2, CORES, HALF, A, LANES), BF), V((CORES, 120, A, LANES), BF),
            V((CORES, 64, A, ALLVEC), BF), V((HALF, A, ALLVEC), F32), V((2, HALF, A, ALLVEC), BF),
            V((2, 3, 16, A, ALLVEC), BF), V((16, A, ALLVEC), F32), V((2, 16, A, ALLVEC), BF),
            V((2, 3, 4, A, ALLVEC), BF), V((4, A, ALLVEC), F32), V((2, 4, A, ALLVEC), BF),
            V((2, 7, A, ALLVEC), BF), V((2, HALF, A, ALLVEC), BF), V((2, CORES, HALF, A, LANES), BF),
            dma((2,)), dma((2,)), dma((2,)), dma((2, 2, 13)), dma((2, 2, 9)), dma((2,)), dma((2,)),
        ],
        compiler_params=pltpu.CompilerParams(has_side_effects=True, vmem_limit_bytes=56 * 2**20),
    )(amplitudes, cholesky)
    return pl.pallas_call(
        unshuffle,
        grid=(TILES // GRP,),
        out_shape=jax.ShapeDtypeStruct(amplitudes.shape, BF),
        in_specs=[pl.BlockSpec((2, GRP, A, LANES), lambda m: (0, m, 0, 0))],
        out_specs=pl.BlockSpec((K, 2, A, 128), lambda m: (0, 0, 0, m)),
    )(landed)


def solution(mesh):
    in_specs = (P("chol", None, "tile", None), P(None, "tile", "chol"))
    out_specs = P("chol", None, "tile", None)
    return jax.shard_map(shards, mesh=mesh, in_specs=in_specs, out_specs=out_specs, check_vma=False)
```

```python
import jax
import jax.numpy as jnp
from jax import lax
from jax.experimental import pallas as pl
from jax.experimental.pallas import tpu as pltpu
from jax.sharding import PartitionSpec as P

MESH = pl.DeviceIdType.MESH
BF, F32 = jnp.bfloat16, jnp.float32
K, VEC = 60, 448
COLS, DEPTH = 16, 8
CUTS, CUT = 5, 12
WIDE = CUT * 64
SUBS, SUB = 4, 15
MAIN, EDGE = 384, 128


def kernel(t_ref, l_ref, out_ref, slab_a, slab_b, slab_c, edge, edge_in, send1, recv1, part, rs_a, rs_bc, rb_a, rb_bc,
           inter_a, inter_bc, send2, recv2, staged, own_sem, swap_send, edge_sem, ring_send, ring_recv, t_send, t_recv,
           sum_send, sum_recv, share_send, share_recv, r_send, r_recv, out_sem):
    me, core = lax.axis_index("tile"), lax.axis_index("chol")
    w, z = me // DEPTH, lax.rem(me, DEPTH)
    y, x = w // 4, lax.rem(w, 4)
    slabs = (slab_a, slab_b, slab_c)

    def plane(q):
        return lax.rem(y + q // 4, 4) * 4 + lax.rem(x + lax.rem(q, 4), 4)

    def level(d):
        return lax.rem(z + d + DEPTH, DEPTH)

    def remote(src, dst, send_sem, recv_sem, tile, to_core):
        return pltpu.make_async_remote_copy(src_ref=src, dst_ref=dst, send_sem=send_sem, recv_sem=recv_sem,
                                            device_id=(tile, to_core), device_id_type=MESH)

    def wait_bytes(ref, sem):
        pltpu.make_async_copy(ref, ref, sem).wait()

    barrier = pltpu.get_barrier_semaphore()

    def greet(q, _):
        pl.semaphore_signal(barrier, inc=1, device_id=(plane(q // 2) * DEPTH + z, lax.rem(core + q, 2)),
                            device_id_type=MESH)
        return 0
    lax.fori_loop(1, 2 * COLS, greet, 0)
    for d in (-1, 1):
        pl.semaphore_signal(barrier, inc=1, device_id=(w * DEPTH + level(d), core), device_id_type=MESH)

    def vectors(own, where, sem):
        def begin():
            for half in range(2):
                src = l_ref.at[pl.ds(half * K, K), :, pl.ds(0, MAIN)]
                if half == own:
                    pltpu.make_async_copy(src, where.at[:, z], sem).start()
                else:
                    remote(src, where.at[:, z], swap_send.at[0], sem, me, 1 - core).start()
        pl.when(core == own)(begin)

    row = lax.broadcasted_iota(jnp.int32, (VEC - MAIN, EDGE), 0)
    column = lax.broadcasted_iota(jnp.int32, (VEC - MAIN, EDGE), 1)
    place = (column == row + (VEC - MAIN) * core).astype(BF)
    tail = jnp.dot(l_ref[:, :, MAIN:].reshape(2 * K * 8, VEC - MAIN), place, preferred_element_type=F32)
    edge[...] = tail.astype(BF).reshape(2 * K, 8, EDGE)

    pl.semaphore_wait(barrier, 2 * COLS + 1)

    vectors(0, slab_a, own_sem.at[0])
    vectors(1, slab_b, own_sem.at[1])
    to_sibling = remote(edge.at[pl.ds((1 - core) * K, K)], edge_in, edge_sem.at[0], edge_sem.at[1], me, 1 - core)
    to_sibling.start()

    sent = []

    def ring(p, hop):
        slab = slabs[p]
        for sub in range(SUBS):
            for way in range(2):
                if hop == 3 and sub % 2 != way:
                    continue
                if hop:
                    arrived(p, sub, way, hop - 1)
                step = -hop if way == 0 else hop
                block = slab.at[pl.ds(sub * SUB, SUB), level(step)]
                n = ((p * SUBS + sub) * 2 + way) * 4 + hop
                copy = remote(block, block, ring_send.at[n], ring_recv.at[n],
                              w * DEPTH + level(1 if way == 0 else -1), core)
                copy.start()
                sent.append(copy)

    def arrived(p, sub, way, hop):
        step = -1 - hop if way == 0 else 1 + hop
        n = ((p * SUBS + sub) * 2 + way) * 4 + hop
        wait_bytes(slabs[p].at[pl.ds(sub * SUB, SUB), level(step)], ring_recv.at[n])

    def last(p):
        for sub in range(SUBS):
            arrived(p, sub, 1 - sub % 2, 2)
            arrived(p, sub, sub % 2, 3)

    low = lax.broadcasted_iota(jnp.int32, (16, 128), 1) < 64

    def halves(first, second):
        return (jnp.where(low, first, pltpu.roll(second, 64, 1)), jnp.where(low, pltpu.roll(first, 64, 1), second))

    def shuffle(n):
        def lane_tile(m, _):
            lanes = pl.ds(pl.multiple_of(m * 128, 128), 128)
            for pair in range(CUT // 2):
                k = n * CUT + 2 * pair
                for side, block in enumerate(halves(t_ref[k, :, lanes].astype(F32), t_ref[k + 1, :, lanes].astype(F32))):
                    send1[n, 2 * m + side, :, pair * 128:(pair + 1) * 128] = block.astype(BF)
            return 0
        lax.fori_loop(0, COLS // 2, lane_tile, 0)

    def unshuffle(n):
        def lane_tile(m, _):
            lanes = pl.ds(pl.multiple_of(m * 128, 128), 128)
            for pair in range(CUT // 2):
                here = slice(pair * 128, (pair + 1) * 128)
                k = n * CUT + 2 * pair
                for side, block in enumerate(halves(recv2[n, 2 * m, :, here].astype(F32),
                                                    recv2[n, 2 * m + 1, :, here].astype(F32))):
                    staged[k + side, :, lanes] = block.astype(BF)
            return 0
        lax.fori_loop(0, COLS // 2, lane_tile, 0)

    def exchange(n, send, recv, send_sem, recv_sem):
        pltpu.make_async_copy(send.at[n, w], recv.at[n, w], recv_sem.at[n]).start()

        def one(q, _):
            to = plane(q)
            remote(send.at[n, to], recv.at[n, w], send_sem.at[n], recv_sem.at[n], to * DEPTH + z, core).start()
            return 0
        lax.fori_loop(1, COLS, one, 0)

    def multiply1(slab, width, rs, lo):
        total = None
        for n in range(CUTS):
            term = jnp.dot(recv1[n].reshape(256, WIDE), slab[n * CUT:(n + 1) * CUT].reshape(WIDE, width),
                           preferred_element_type=F32)
            total = term if total is None else total + term
        total = total.reshape(COLS, 2, 8, width)
        part[:, :, :, lo:lo + width] = total
        rs[:, :, :, lo:lo + width] = total.astype(BF)

    def add_up(i, rs, rb):
        def one(q, _):
            to, to_core = plane(q // 2), lax.rem(core + q, 2)
            remote(rs.at[to, to_core], rb.at[q - 1], sum_send.at[i], sum_recv.at[i], to * DEPTH + z, to_core).start()
            return 0
        lax.fori_loop(1, 2 * COLS, one, 0)

    def share(i, rb, inter, width):
        wait_bytes(rb, sum_recv.at[i])
        total = part[w, core, :, :width]
        for n in range(2 * COLS - 1):
            total = total + rb[n].astype(F32)
        inter[w, core] = total.astype(BF)

        def one(q, _):
            to, to_core = plane(q // 2), lax.rem(core + q, 2)
            block = inter.at[w, core]
            remote(block, block, share_send.at[i], share_recv.at[i], to * DEPTH + z, to_core).start()
            return 0
        lax.fori_loop(1, 2 * COLS, one, 0)

    def multiply2(n):
        def times(rows, slab, width):
            return lax.dot_general(rows.reshape(256, width), slab[n * CUT:(n + 1) * CUT].reshape(WIDE, width),
                                   (((1,), (1,)), ((), ())), preferred_element_type=F32)
        total = times(inter_a[...], slab_a, MAIN)
        total = total + times(inter_bc[:, :, :, :MAIN], slab_b, MAIN)
        total = total + times(inter_bc[:, :, :, MAIN:], slab_c, EDGE)
        send2[n] = total.astype(BF).reshape(COLS, 16, WIDE)

    wait_bytes(slab_a.at[:, z], own_sem.at[0])
    ring(0, 0)
    for n in range(CUTS):
        shuffle(n)
        exchange(n, send1, recv1, t_send, t_recv)
    to_sibling.wait_recv()

    def merge(k, _):
        slab_c[k, z] = (edge[core * K + k].astype(F32) + edge_in[k].astype(F32)).astype(BF)
        return 0
    lax.fori_loop(0, K, merge, 0)
    ring(0, 1)
    ring(0, 2)
    ring(0, 3)
    wait_bytes(slab_b.at[:, z], own_sem.at[1])
    ring(1, 0)
    ring(2, 0)
    last(0)
    for n in range(CUTS):
        wait_bytes(recv1.at[n], t_recv.at[n])
    multiply1(slab_a, MAIN, rs_a, 0)
    add_up(0, rs_a, rb_a)
    ring(1, 1)
    ring(2, 1)
    share(0, rb_a, inter_a, MAIN)
    ring(1, 2)
    ring(2, 2)
    ring(1, 3)
    ring(2, 3)
    last(1)
    multiply1(slab_b, MAIN, rs_bc, 0)
    last(2)
    multiply1(slab_c, EDGE, rs_bc, MAIN)
    add_up(1, rs_bc, rb_bc)
    wait_bytes(rb_a, share_recv.at[0])
    share(1, rb_bc, inter_bc, MAIN + EDGE)
    wait_bytes(rb_bc, share_recv.at[1])
    for n in range(CUTS):
        multiply2(n)
        exchange(n, send2, recv2, r_send, r_recv)
    for n in range(CUTS):
        wait_bytes(recv2.at[n], r_recv.at[n])
        unshuffle(n)
        pltpu.make_async_copy(staged.at[pl.ds(n * CUT, CUT)], out_ref.at[pl.ds(n * CUT, CUT)], out_sem.at[n]).start()

    for copy in sent + [to_sibling]:
        copy.wait_send()
    wait_bytes(slab_a.at[:, z], swap_send.at[0])
    for n in range(CUTS):
        wait_bytes(recv1.at[n, pl.ds(0, COLS - 1)], t_send.at[n])
        wait_bytes(recv2.at[n, pl.ds(0, COLS - 1)], r_send.at[n])
    for i, rb in enumerate((rb_a, rb_bc)):
        wait_bytes(rb, sum_send.at[i])
        wait_bytes(rb, share_send.at[i])
    for n in range(CUTS):
        wait_bytes(staged.at[pl.ds(n * CUT, CUT)], out_sem.at[n])


def shards(amplitudes, cholesky):
    vmem = pl.BlockSpec(memory_space=pltpu.VMEM)
    dma, V = pltpu.SemaphoreType.DMA, pltpu.VMEM
    both = MAIN + EDGE
    out = pl.pallas_call(
        kernel,
        out_shape=jax.ShapeDtypeStruct((K, 16, 1024), BF),
        in_specs=[vmem, vmem],
        out_specs=pl.BlockSpec(memory_space=pl.ANY),
        scratch_shapes=[
            V((K, DEPTH, 8, MAIN), BF), V((K, DEPTH, 8, MAIN), BF), V((K, DEPTH, 8, EDGE), BF),
            V((2 * K, 8, EDGE), BF), V((K, 8, EDGE), BF),
            V((CUTS, COLS, 16, WIDE), BF), V((CUTS, COLS, 16, WIDE), BF),
            V((COLS, 2, 8, both), F32), V((COLS, 2, 8, MAIN), BF), V((COLS, 2, 8, both), BF),
            V((2 * COLS - 1, 8, MAIN), BF), V((2 * COLS - 1, 8, both), BF),
            V((COLS, 2, 8, MAIN), BF), V((COLS, 2, 8, both), BF),
            V((CUTS, COLS, 16, WIDE), BF), V((CUTS, COLS, 16, WIDE), BF), V((K, 16, 1024), BF),
            dma((2,)), dma((1,)), dma((2,)), dma((96,)), dma((96,)), dma((CUTS,)), dma((CUTS,)),
            dma((2,)), dma((2,)), dma((2,)), dma((2,)), dma((CUTS,)), dma((CUTS,)), dma((CUTS,)),
        ],
        compiler_params=pltpu.CompilerParams(has_side_effects=True, collective_id=0, vmem_limit_bytes=56 * 2**20),
    )(amplitudes.reshape(K, 16, 1024), cholesky)
    return out.reshape(amplitudes.shape)


def solution(mesh):
    in_specs = (P("chol", None, "tile", None), P(None, "tile", "chol"))
    out_specs = P("chol", None, "tile", None)
    return jax.shard_map(shards, mesh=mesh, in_specs=in_specs, out_specs=out_specs, check_vma=False)
```

```python
import jax
import jax.numpy as jnp
from jax import lax
from jax.experimental import pallas as pl
from jax.experimental.pallas import tpu as pltpu
from jax.sharding import PartitionSpec as P

MESH = pl.DeviceIdType.MESH
BF, F32 = jnp.bfloat16, jnp.float32
K, VEC = 60, 448
COLS, DEPTH = 16, 8
CUTS, CUT = 5, 12
WIDE = CUT * 64
SUBS, SUB = 4, 15
MAIN, EDGE = 384, 128


def kernel(t_hbm, l_hbm, out_ref, t_ref, l_ref, slab_a, slab_b, slab_c, edge, edge_in, send1, recv1, part_a, part_b, part_c,
           rs_a, rs_b, rs_c, rb_a, rb_b, rb_c, inter_a, inter_b, inter_c, send2, recv2, own_sem, swap_send, edge_sem,
           ring_send, ring_recv, t_send, t_recv, sum_send, sum_recv, share_send, share_recv, r_send, r_recv, in_sem):
    load_l = pltpu.make_async_copy(l_hbm, l_ref, in_sem.at[0])
    load_l.start()
    load_t = pltpu.make_async_copy(t_hbm, t_ref, in_sem.at[1])
    load_t.start()
    me, core = lax.axis_index("tile"), lax.axis_index("chol")
    w, z = me // DEPTH, lax.rem(me, DEPTH)
    y, x = w // 4, lax.rem(w, 4)
    slabs, widths = (slab_a, slab_b, slab_c), (MAIN, MAIN, EDGE)
    parts, rss, rbs, inters = (part_a, part_b, part_c), (rs_a, rs_b, rs_c), (rb_a, rb_b, rb_c), (inter_a, inter_b, inter_c)

    def plane(q):
        return lax.rem(y + q // 4, 4) * 4 + lax.rem(x + lax.rem(q, 4), 4)

    def level(d):
        return lax.rem(z + d + DEPTH, DEPTH)

    def remote(src, dst, send_sem, recv_sem, tile, to_core):
        return pltpu.make_async_remote_copy(src_ref=src, dst_ref=dst, send_sem=send_sem, recv_sem=recv_sem,
                                            device_id=(tile, to_core), device_id_type=MESH)

    def wait_bytes(ref, sem):
        pltpu.make_async_copy(ref, ref, sem).wait()

    barrier = pltpu.get_barrier_semaphore()

    def greet(q, _):
        pl.semaphore_signal(barrier, inc=1, device_id=(plane(q // 2) * DEPTH + z, lax.rem(core + q, 2)),
                            device_id_type=MESH)
        return 0
    lax.fori_loop(1, 2 * COLS, greet, 0)
    for d in (-1, 1):
        pl.semaphore_signal(barrier, inc=1, device_id=(w * DEPTH + level(d), core), device_id_type=MESH)

    def vectors(own, where, sem):
        def begin():
            for half in range(2):
                src = l_hbm.at[pl.ds(half * K, K), :, pl.ds(0, MAIN)]
                if half == own:
                    pltpu.make_async_copy(src, where.at[:, z], sem).start()
                else:
                    remote(src, where.at[:, z], swap_send.at[0], sem, me, 1 - core).start()
        pl.when(core == own)(begin)

    pl.semaphore_wait(barrier, 2 * COLS + 1)

    vectors(0, slab_a, own_sem.at[0])
    vectors(1, slab_b, own_sem.at[1])
    sent = []

    def ring(p, hop):
        slab = slabs[p]
        for sub in range(SUBS):
            for way in range(2):
                if hop == 3 and sub % 2 != way:
                    continue
                if hop:
                    arrived(p, sub, way, hop - 1)
                step = -hop if way == 0 else hop
                block = slab.at[pl.ds(sub * SUB, SUB), level(step)]
                n = ((p * SUBS + sub) * 2 + way) * 4 + hop
                copy = remote(block, block, ring_send.at[n], ring_recv.at[n],
                              w * DEPTH + level(1 if way == 0 else -1), core)
                copy.start()
                sent.append(copy)

    def arrived(p, sub, way, hop):
        step = -1 - hop if way == 0 else 1 + hop
        n = ((p * SUBS + sub) * 2 + way) * 4 + hop
        wait_bytes(slabs[p].at[pl.ds(sub * SUB, SUB), level(step)], ring_recv.at[n])

    def last(p):
        for sub in range(SUBS):
            arrived(p, sub, 1 - sub % 2, 2)
            arrived(p, sub, sub % 2, 3)

    low = lax.broadcasted_iota(jnp.int32, (16, 128), 1) < 64

    def halves(first, second):
        return (jnp.where(low, first, pltpu.roll(second, 64, 1)), jnp.where(low, pltpu.roll(first, 64, 1), second))

    def shuffle(n):
        def lane_tile(m, _):
            lanes = pl.ds(pl.multiple_of(m * 128, 128), 128)
            for pair in range(CUT // 2):
                k = n * CUT + 2 * pair
                for side, block in enumerate(halves(t_ref[k, :, lanes].astype(F32), t_ref[k + 1, :, lanes].astype(F32))):
                    send1[n, 2 * m + side, :, pair * 128:(pair + 1) * 128] = block.astype(BF)
            return 0
        lax.fori_loop(0, COLS // 2, lane_tile, 0)

    def unshuffle(n):
        def lane_tile(m, _):
            lanes = pl.ds(pl.multiple_of(m * 128, 128), 128)
            for pair in range(CUT // 2):
                here = slice(pair * 128, (pair + 1) * 128)
                k = n * CUT + 2 * pair
                for side, block in enumerate(halves(recv2[n, 2 * m, :, here].astype(F32),
                                                    recv2[n, 2 * m + 1, :, here].astype(F32))):
                    out_ref[k + side, :, lanes] = block.astype(BF)
            return 0
        lax.fori_loop(0, COLS // 2, lane_tile, 0)

    def exchange(n, send, recv, send_sem, recv_sem):
        pltpu.make_async_copy(send.at[n, w], recv.at[n, w], recv_sem.at[n]).start()

        def one(q, _):
            to = plane(q)
            remote(send.at[n, to], recv.at[n, w], send_sem.at[n], recv_sem.at[n], to * DEPTH + z, core).start()
            return 0
        lax.fori_loop(1, COLS, one, 0)

    def multiply1(p):
        slab, width = slabs[p], widths[p]
        total = None
        for n in range(CUTS):
            term = jnp.dot(recv1[n].reshape(256, WIDE), slab[n * CUT:(n + 1) * CUT].reshape(WIDE, width),
                           preferred_element_type=F32)
            total = term if total is None else total + term
        total = total.reshape(COLS, 2, 8, width)
        parts[p][...] = total
        rss[p][...] = total.astype(BF)

    def add_up(p):
        def one(q, _):
            to, to_core = plane(q // 2), lax.rem(core + q, 2)
            remote(rss[p].at[to, to_core], rbs[p].at[q - 1], sum_send.at[p], sum_recv.at[p], to * DEPTH + z,
                   to_core).start()
            return 0
        lax.fori_loop(1, 2 * COLS, one, 0)

    def share(p):
        wait_bytes(rbs[p], sum_recv.at[p])
        total = parts[p][w, core]
        for n in range(2 * COLS - 1):
            total = total + rbs[p][n].astype(F32)
        inters[p][w, core] = total.astype(BF)

        def one(q, _):
            to, to_core = plane(q // 2), lax.rem(core + q, 2)
            block = inters[p].at[w, core]
            remote(block, block, share_send.at[p], share_recv.at[p], to * DEPTH + z, to_core).start()
            return 0
        lax.fori_loop(1, 2 * COLS, one, 0)

    def multiply2(n):
        total = None
        for p in range(3):
            rows = slabs[p][n * CUT:(n + 1) * CUT].reshape(WIDE, widths[p])
            term = lax.dot_general(inters[p][...].reshape(256, widths[p]), rows, (((1,), (1,)), ((), ())),
                                   preferred_element_type=F32)
            total = term if total is None else total + term
        send2[n] = total.astype(BF).reshape(COLS, 16, WIDE)

    wait_bytes(slab_a.at[:, z], own_sem.at[0])
    ring(0, 0)
    load_l.wait()
    row = lax.broadcasted_iota(jnp.int32, (VEC - MAIN, EDGE), 0)
    column = lax.broadcasted_iota(jnp.int32, (VEC - MAIN, EDGE), 1)
    place = (column == row + (VEC - MAIN) * core).astype(BF)
    tail = jnp.dot(l_ref[:, :, MAIN:].reshape(2 * K * 8, VEC - MAIN), place, preferred_element_type=F32)
    edge[...] = tail.astype(BF).reshape(2 * K, 8, EDGE)
    to_sibling = remote(edge.at[pl.ds((1 - core) * K, K)], edge_in, edge_sem.at[0], edge_sem.at[1], me, 1 - core)
    to_sibling.start()
    load_t.wait()
    for n in range(CUTS):
        shuffle(n)
        exchange(n, send1, recv1, t_send, t_recv)
    to_sibling.wait_recv()

    def merge(k, _):
        slab_c[k, z] = (edge[core * K + k].astype(F32) + edge_in[k].astype(F32)).astype(BF)
        return 0
    lax.fori_loop(0, K, merge, 0)
    ring(0, 1)
    ring(0, 2)
    ring(0, 3)
    wait_bytes(slab_b.at[:, z], own_sem.at[1])
    ring(1, 0)
    ring(2, 0)
    last(0)
    for n in range(CUTS):
        wait_bytes(recv1.at[n], t_recv.at[n])
    multiply1(0)
    add_up(0)
    ring(1, 1)
    ring(2, 1)
    share(0)
    ring(1, 2)
    ring(2, 2)
    ring(1, 3)
    ring(2, 3)
    last(1)
    multiply1(1)
    add_up(1)
    last(2)
    multiply1(2)
    add_up(2)
    share(1)
    share(2)
    for p in range(3):
        wait_bytes(rbs[p], share_recv.at[p])
    for n in range(CUTS):
        multiply2(n)
        exchange(n, send2, recv2, r_send, r_recv)
    for n in range(CUTS):
        wait_bytes(recv2.at[n], r_recv.at[n])
        unshuffle(n)

    for copy in sent + [to_sibling]:
        copy.wait_send()
    wait_bytes(slab_a.at[:, z], swap_send.at[0])
    for n in range(CUTS):
        wait_bytes(recv1.at[n, pl.ds(0, COLS - 1)], t_send.at[n])
        wait_bytes(recv2.at[n, pl.ds(0, COLS - 1)], r_send.at[n])
    for p in range(3):
        wait_bytes(rbs[p], sum_send.at[p])
        wait_bytes(rbs[p], share_send.at[p])


def shards(amplitudes, cholesky):
    dma, V = pltpu.SemaphoreType.DMA, pltpu.VMEM
    widths = (MAIN, MAIN, EDGE)
    out = pl.pallas_call(
        kernel,
        out_shape=jax.ShapeDtypeStruct((K, 16, 1024), BF),
        in_specs=[pl.BlockSpec(memory_space=pl.ANY)] * 2,
        out_specs=pl.BlockSpec(memory_space=pltpu.VMEM),
        scratch_shapes=[
            V((K, 16, 1024), BF), V((2 * K, 8, VEC), BF),
            *[V((K, DEPTH, 8, n), BF) for n in widths],
            V((2 * K, 8, EDGE), BF), V((K, 8, EDGE), BF),
            V((CUTS, COLS, 16, WIDE), BF), V((CUTS, COLS, 16, WIDE), BF),
            *[V((COLS, 2, 8, n), F32) for n in widths], *[V((COLS, 2, 8, n), BF) for n in widths],
            *[V((2 * COLS - 1, 8, n), BF) for n in widths], *[V((COLS, 2, 8, n), BF) for n in widths],
            V((CUTS, COLS, 16, WIDE), BF), V((CUTS, COLS, 16, WIDE), BF),
            dma((2,)), dma((1,)), dma((2,)), dma((96,)), dma((96,)), dma((CUTS,)), dma((CUTS,)),
            dma((3,)), dma((3,)), dma((3,)), dma((3,)), dma((CUTS,)), dma((CUTS,)), dma((2,)),
        ],
        compiler_params=pltpu.CompilerParams(has_side_effects=True, collective_id=0, vmem_limit_bytes=44 * 2**20),
    )(amplitudes.reshape(K, 16, 1024), cholesky)
    return out.reshape(amplitudes.shape)


def solution(mesh):
    in_specs = (P("chol", None, "tile", None), P(None, "tile", "chol"))
    out_specs = P("chol", None, "tile", None)
    return jax.shard_map(shards, mesh=mesh, in_specs=in_specs, out_specs=out_specs, check_vma=False)
```

```python
import jax
import jax.numpy as jnp
from jax import lax
from jax.experimental import pallas as pl
from jax.experimental.pallas import tpu as pltpu
from jax.sharding import PartitionSpec as P

MESH = pl.DeviceIdType.MESH
BF, F32 = jnp.bfloat16, jnp.float32
K, VEC = 60, 448
COLS, DEPTH = 16, 8
CUTS, CUT = 5, 12
SENDERS = COLS + DEPTH
MAIN, EDGE = 384, 128


PEERS, BLOCKS = (COLS, DEPTH), (DEPTH, COLS)


def kernel(t_hbm, l_hbm, out_ref, t_ref, l_ref, slab_a, slab_b, slab_c, edge, edge_in, send, t_in, r_in,
           rs_a, rs_b, rs_c, rb_a, rb_b, rb_c, mine_a, mine_b, mine_c, inter_a, inter_b, inter_c, own_sem, swap_send,
           edge_sem, ring_send, ring_recv, t_send, t_recv, sum_send, sum_recv, share_send, share_recv, r_send, r_recv,
           in_sem):
    load_l = pltpu.make_async_copy(l_hbm, l_ref, in_sem.at[0])
    load_l.start()
    load_t = pltpu.make_async_copy(t_hbm, t_ref, in_sem.at[1])
    load_t.start()
    me, core = lax.axis_index("tile"), lax.axis_index("chol")
    w, z = me // DEPTH, lax.rem(me, DEPTH)
    y, x = w // 4, lax.rem(w, 4)
    slabs, widths = (slab_a, slab_b, slab_c), (MAIN, MAIN, EDGE)
    rss, rbs, mines, inters = (rs_a, rs_b, rs_c), (rb_a, rb_b, rb_c), (mine_a, mine_b, mine_c), (inter_a, inter_b, inter_c)

    def plane(q):
        return lax.rem(y + q // 4, 4) * 4 + lax.rem(x + lax.rem(q, 4), 4)

    def level(d):
        return lax.rem(z + d + DEPTH, DEPTH)

    def near(dx, dy):
        return lax.rem(y + dy + 4, 4) * 4 + lax.rem(x + dx + 4, 4)

    def in_slab(column):
        return lax.rem(column, 2) * 8 + column // 2

    def remote(src, dst, send_sem, recv_sem, tile, to_core):
        return pltpu.make_async_remote_copy(src_ref=src, dst_ref=dst, send_sem=send_sem, recv_sem=recv_sem,
                                            device_id=(tile, to_core), device_id_type=MESH)

    def wait_bytes(ref, sem):
        pltpu.make_async_copy(ref, ref, sem).wait()

    def each(lo, hi, one):
        def step(q, _):
            one(q)
            return 0
        lax.fori_loop(lo, hi, step, 0)

    barrier = pltpu.get_barrier_semaphore()

    def greet(tile, to_core):
        pl.semaphore_signal(barrier, inc=1, device_id=(tile, to_core), device_id_type=MESH)

    @pl.when(core == 0)
    def _():
        each(1, COLS, lambda q: greet(plane(q) * DEPTH + z, 0))
        each(0, COLS, lambda q: greet(plane(q) * DEPTH + z, 1))
        each(1, DEPTH, lambda d: greet(w * DEPTH + level(d), 1))
        for d in (-1, 1):
            greet(w * DEPTH + level(d), 0)
        pl.semaphore_wait(barrier, 2 * COLS + DEPTH)

    @pl.when(core == 1)
    def _():
        each(0, DEPTH, lambda d: greet(w * DEPTH + level(d), 0))
        each(1, DEPTH, lambda d: greet(w * DEPTH + level(d), 1))
        each(1, COLS, lambda q: greet(plane(q) * DEPTH + z, 0))
        for dx, dy in ((1, 0), (-1, 0), (0, 1), (0, -1)):
            greet(near(dx, dy) * DEPTH + z, 1)
        pl.semaphore_wait(barrier, COLS + 2 * DEPTH + 2)

    low = lax.broadcasted_iota(jnp.int32, (16, 128), 1) < 64
    granule = lax.broadcasted_iota(jnp.int32, (16, 128), 1) // 8

    def halves(first, second):
        return (jnp.where(low, first, pltpu.roll(second, 64, 1)), jnp.where(low, pltpu.roll(first, 64, 1), second))

    def swap(blocks):
        for bit in (1, 2, 4):
            take = (granule & bit) != 0
            new = list(blocks)
            for i in range(8):
                if not i & bit:
                    first, second = blocks[i], blocks[i | bit]
                    new[i] = jnp.where(take, pltpu.roll(second, 8 * bit, 1), first)
                    new[i | bit] = jnp.where(take, second, pltpu.roll(first, 128 - 8 * bit, 1))
            blocks = new
        return blocks

    def tile_of(m):
        return pl.ds(pl.multiple_of(m * 128, 128), 128)

    def run(c):
        peers, blocks = PEERS[c], BLOCKS[c]
        wide = CUT * 8 * blocks

        def piece_of(buffer, n, place):
            if c == 0:
                return buffer.at[n, place // 2, :, pl.ds(pl.multiple_of(lax.rem(place, 2) * wide, 128), wide)]
            return buffer.at[n, place]

        own = z if c == 0 else in_slab(w)
        place_in_rows = w if c == 0 else z
        sent = []

        def peer(q):
            return plane(q) if c == 0 else level(q)

        def tile(q):
            return plane(q) * DEPTH + z if c == 0 else w * DEPTH + level(q)

        def vectors(owner, where, sem):
            if c != owner:
                return
            pltpu.make_async_copy(l_hbm.at[pl.ds(c * K, K), :, pl.ds(0, MAIN)], where.at[:, own], sem).start()
            theirs = in_slab(w) if c == 0 else z
            remote(l_hbm.at[pl.ds((1 - c) * K, K), :, pl.ds(0, MAIN)], where.at[:, theirs], swap_send.at[0], sem, me,
                   1 - c).start()

        def pass_on(p, rows, block, n, to):
            piece = slabs[p].at[rows, block]
            copy = remote(piece, piece, ring_send.at[n], ring_recv.at[n], to, c)
            copy.start()
            sent.append(copy)

        def z_ring(p, hop):
            for sub in range(4):
                for way in range(2):
                    if hop == 3 and sub % 2 != way:
                        continue
                    if hop:
                        z_arrived(p, sub, way, hop - 1)
                    pass_on(p, pl.ds(sub * 15, 15), level(-hop if way == 0 else hop), ((p * 4 + sub) * 2 + way) * 4 + hop,
                            w * DEPTH + level(1 if way == 0 else -1))

        def z_arrived(p, sub, way, hop):
            step = -1 - hop if way == 0 else 1 + hop
            wait_bytes(slabs[p].at[pl.ds(sub * 15, 15), level(step)], ring_recv.at[((p * 4 + sub) * 2 + way) * 4 + hop])

        def xy_number(p, half, a, b):
            return (p * 2 + half) * 16 + a % 4 * 4 + b % 4

        def xy_block(half, a, b):
            return in_slab(near(*((a, b) if half == 0 else (b, a))))

        def xy_send(p, half, second, way, a, b):
            to = near(way, 0) if (half == 0) != second else near(0, way)
            n = xy_number(p, half, a, b - way) if second else xy_number(p, half, a - way, b)
            pass_on(p, pl.ds(half * 30, 30), xy_block(half, a, b), n, to * DEPTH + z)

        def xy_arrived(p, half, a, b):
            wait_bytes(slabs[p].at[pl.ds(half * 30, 30), xy_block(half, a, b)], ring_recv.at[xy_number(p, half, a, b)])

        def xy_ring(p, stage):
            for half in range(2):
                if stage == 0:
                    for second in (False, True):
                        for way in (1, -1):
                            xy_send(p, half, second, way, 0, 0)
                if stage == 1:
                    for a in (3, 1):
                        xy_arrived(p, half, a, 0)
                        if a == 3:
                            xy_send(p, half, False, 1, a, 0)
                        for way in (1, -1):
                            xy_send(p, half, True, way, a, 0)
                if stage == 2:
                    xy_arrived(p, half, 0, 3)
                    xy_send(p, half, True, 1, 0, 3)
                    xy_arrived(p, half, 2, 0)
                    for way in (1, -1):
                        xy_send(p, half, True, way, 2, 0)
                if stage == 3:
                    for a in (3, 1):
                        xy_arrived(p, half, a, 1)
                        xy_send(p, half, True, -1, a, 1)
                    xy_arrived(p, half, 2, 3)
                    xy_send(p, half, True, 1, 2, 3)

        def last(p):
            if c == 0:
                for sub in range(4):
                    z_arrived(p, sub, 1 - sub % 2, 2)
                    z_arrived(p, sub, sub % 2, 3)
            else:
                for half in range(2):
                    for a, b in ((0, 1), (3, 3), (1, 3), (2, 1), (0, 2), (3, 2), (1, 2), (2, 2)):
                        xy_arrived(p, half, a, b)

        ring = z_ring if c == 0 else xy_ring

        def shuffle(n):
            if c == 0:
                def lane_tile(m):
                    for pair in range(CUT // 2):
                        k = n * CUT + 2 * pair
                        for side, block in enumerate(halves(t_ref[k, :, tile_of(m)].astype(F32),
                                                            t_ref[k + 1, :, tile_of(m)].astype(F32))):
                            at = side * wide + pair * 128
                            send[n, m, :, at:at + 128] = block.astype(BF)
                each(0, COLS // 2, lane_tile)
            else:
                def one_row(k):
                    for i, block in enumerate(swap([t_ref[n * CUT + k, :, m * 128:(m + 1) * 128].astype(F32)
                                                    for m in range(8)])):
                        send[n, i, :, tile_of(k)] = block.astype(BF)
                each(0, CUT, one_row)

        def unshuffle(n):
            if c == 0:
                def lane_tile(m):
                    for pair in range(CUT // 2):
                        lo, hi, k = pair * 128, wide + pair * 128, n * CUT + 2 * pair
                        for side, block in enumerate(halves(r_in[n, m, :, lo:lo + 128].astype(F32),
                                                            r_in[n, m, :, hi:hi + 128].astype(F32))):
                            out_ref[k + side, :, tile_of(m)] = block.astype(BF)
                each(0, COLS // 2, lane_tile)
            else:
                def one_row(k):
                    for m, block in enumerate(swap([r_in[n, i, :, tile_of(k)].astype(F32) for i in range(8)])):
                        out_ref[n * CUT + k, :, m * 128:(m + 1) * 128] = block.astype(BF)
                each(0, CUT, one_row)

        def exchange(n, into, send_sem, recv_sem):
            here = place_in_rows
            pltpu.make_async_copy(piece_of(send, n, here), piece_of(into, n, here), recv_sem.at[n]).start()
            each(1, peers, lambda q: remote(piece_of(send, n, peer(q)), piece_of(into, n, here), send_sem.at[n],
                                            recv_sem.at[n], tile(q), c).start())

        def all_but_one(n):
            if c == 0:
                return t_ref.at[pl.ds(0, COLS - 1), :, pl.ds(0, wide)]
            return t_in.at[n, pl.ds(0, DEPTH - 1)]

        def vectors_of(p, n):
            return slabs[p][n * CUT:(n + 1) * CUT, :blocks].reshape(wide, widths[p])

        def multiply1(p):
            total = None
            for n in range(CUTS):
                if c == 0:
                    rows = jnp.concatenate([t_in[n, :, :, :wide].reshape(128, wide), t_in[n, :, :, wide:].reshape(128, wide)])
                else:
                    rows = t_in[n].reshape(128, wide)
                term = jnp.dot(rows, vectors_of(p, n), preferred_element_type=F32)
                total = term if total is None else total + term
            rss[p][:peers] = total.astype(BF).reshape(peers, 2, 8, widths[p])

        def sums_of(place):
            return in_slab(place) if c == 0 else place

        def add_up(p):
            first = 0 if c == 0 else COLS
            pltpu.make_async_copy(rss[p].at[sums_of(place_in_rows), c], rbs[p].at[first], sum_recv.at[p]).start()

            def one(q):
                n, to_core = q // 2, lax.rem(q + c, 2)
                remote(rss[p].at[sums_of(peer(n)), to_core], rbs[p].at[first + n], sum_send.at[p], sum_recv.at[p], tile(n),
                       to_core).start()
            each(1, 2 * peers, one)

        def share(p):
            wait_bytes(rbs[p].at[pl.ds(0, SENDERS)], sum_recv.at[p])
            total = rbs[p][0].astype(F32)
            for n in range(1, SENDERS):
                total = total + rbs[p][n].astype(F32)
            mines[p][...] = total.astype(BF)
            pltpu.make_async_copy(mines[p], inters[p].at[place_in_rows, c], share_recv.at[p]).start()
            each(1 if c == 0 else 0, COLS, lambda q: remote(
                mines[p], inters[p].at[w, c], share_send.at[p], share_recv.at[p], plane(q) * DEPTH + z, 0).start())
            each(1 if c == 1 else 0, DEPTH, lambda d: remote(
                mines[p], inters[p].at[z, c], share_send.at[p], share_recv.at[p], w * DEPTH + level(d), 1).start())

        def multiply2(n):
            total = None
            for p in range(3):
                rows = inters[p][:peers].reshape(peers * 16, widths[p])
                term = lax.dot_general(rows, vectors_of(p, n), (((1,), (1,)), ((), ())), preferred_element_type=F32)
                total = term if total is None else total + term
            if c == 0:
                total = total.astype(BF).reshape(8, 2, 16, wide)
                send[n, :, :, :wide] = total[:, 0]
                send[n, :, :, wide:] = total[:, 1]
            else:
                send[n] = total.astype(BF).reshape(8, 16, wide)

        vectors(0, slab_a, own_sem.at[0])
        vectors(1, slab_b, own_sem.at[1])
        wait_bytes(slab_a.at[:, own], own_sem.at[0])
        ring(0, 0)
        load_l.wait()
        row = lax.broadcasted_iota(jnp.int32, (VEC - MAIN, EDGE), 0)
        column = lax.broadcasted_iota(jnp.int32, (VEC - MAIN, EDGE), 1)
        place = (column == row + (VEC - MAIN) * c).astype(BF)
        tail = jnp.dot(l_ref[:, :, MAIN:].reshape(2 * K * 8, VEC - MAIN), place, preferred_element_type=F32)
        edge[...] = tail.astype(BF).reshape(2 * K, 8, EDGE)
        to_sibling = remote(edge.at[pl.ds((1 - c) * K, K)], edge_in, edge_sem.at[0], edge_sem.at[1], me, 1 - c)
        to_sibling.start()
        load_t.wait()
        for n in range(CUTS):
            shuffle(n)
            exchange(n, t_in, t_send, t_recv)
        to_sibling.wait_recv()

        def merge(k):
            slab_c[k, own] = (edge[c * K + k].astype(F32) + edge_in[k].astype(F32)).astype(BF)
        each(0, K, merge)
        for stage in (1, 2, 3):
            ring(0, stage)
        wait_bytes(slab_b.at[:, own], own_sem.at[1])
        ring(1, 0)
        ring(2, 0)
        last(0)
        for n in range(CUTS):
            wait_bytes(t_in.at[n], t_recv.at[n])
        multiply1(0)
        add_up(0)
        ring(1, 1)
        ring(2, 1)
        share(0)
        for stage in (2, 3):
            ring(1, stage)
            ring(2, stage)
        for n in range(CUTS):
            wait_bytes(all_but_one(n), t_send.at[n])
        last(1)
        multiply1(1)
        add_up(1)
        last(2)
        multiply1(2)
        add_up(2)
        share(1)
        share(2)
        for p in range(3):
            wait_bytes(inters[p].at[pl.ds(0, peers)], share_recv.at[p])
        for n in range(CUTS):
            multiply2(n)
            exchange(n, r_in, r_send, r_recv)
        for n in range(CUTS):
            wait_bytes(r_in.at[n], r_recv.at[n])
            unshuffle(n)

        for copy in sent + [to_sibling]:
            copy.wait_send()
        wait_bytes(slabs[c].at[:, own], swap_send.at[0])
        for n in range(CUTS):
            wait_bytes(all_but_one(n), r_send.at[n])
        for p in range(3):
            wait_bytes(rbs[p].at[pl.ds(0, 2 * peers - 1)], sum_send.at[p])
            wait_bytes(rbs[p].at[pl.ds(0, SENDERS - 1)], share_send.at[p])

    pl.when(core == 0)(lambda: run(0))
    pl.when(core == 1)(lambda: run(1))


def shards(amplitudes, cholesky):
    dma, V = pltpu.SemaphoreType.DMA, pltpu.VMEM
    widths = (MAIN, MAIN, EDGE)
    out = pl.pallas_call(
        kernel,
        out_shape=jax.ShapeDtypeStruct((K, 16, 1024), BF),
        in_specs=[pl.BlockSpec(memory_space=pl.ANY)] * 2,
        out_specs=pl.BlockSpec(memory_space=pltpu.VMEM),
        scratch_shapes=[
            V((K, 16, 1024), BF), V((2 * K, 8, VEC), BF),
            *[V((K, COLS, 8, n), BF) for n in widths],
            V((2 * K, 8, EDGE), BF), V((K, 8, EDGE), BF),
            *[V((CUTS, DEPTH, 16, CUT * 8 * COLS), BF)] * 3,
            *[V((COLS, 2, 8, n), BF) for n in widths], *[V((2 * COLS, 8, n), BF) for n in widths],
            *[V((8, n), BF) for n in widths], *[V((COLS, 2, 8, n), BF) for n in widths],
            dma((2,)), dma((1,)), dma((2,)), dma((96,)), dma((96,)), dma((CUTS,)), dma((CUTS,)),
            dma((3,)), dma((3,)), dma((3,)), dma((3,)), dma((CUTS,)), dma((CUTS,)), dma((2,)),
        ],
        compiler_params=pltpu.CompilerParams(has_side_effects=True, collective_id=0, vmem_limit_bytes=44 * 2**20),
    )(amplitudes.reshape(K, 16, 1024), cholesky)
    return out.reshape(amplitudes.shape)


def solution(mesh):
    in_specs = (P("chol", None, "tile", None), P(None, "tile", "chol"))
    out_specs = P("chol", None, "tile", None)
    return jax.shard_map(shards, mesh=mesh, in_specs=in_specs, out_specs=out_specs, check_vma=False)
```

```python
import jax
import jax.numpy as jnp
from jax import lax
from jax.experimental import pallas as pl
from jax.experimental.pallas import tpu as pltpu
from jax.sharding import PartitionSpec as P

MESH = pl.DeviceIdType.MESH
BF, F32 = jnp.bfloat16, jnp.float32
K, VEC = 60, 448
COLS, DEPTH = 16, 8
CUTS, CUT = 10, 6
SENDERS = COLS + DEPTH
MAIN, EDGE = 384, 128


PEERS, BLOCKS = (COLS, DEPTH), (DEPTH, COLS)


def kernel(t_hbm, l_hbm, out_ref, t_ref, l_ref, slab_a, slab_b, slab_c, edge, edge_in, send, t_in, r_in,
           rs_a, rs_b, rs_c, rb_a, rb_b, rb_c, mine_a, mine_b, mine_c, inter_a, inter_b, inter_c, own_sem, swap_send,
           edge_sem, ring_send, ring_recv, t_send, t_recv, sum_send, sum_recv, share_send, share_recv, r_send, r_recv,
           in_sem):
    load_l = pltpu.make_async_copy(l_hbm, l_ref, in_sem.at[0])
    load_l.start()
    load_t = pltpu.make_async_copy(t_hbm, t_ref, in_sem.at[1])
    load_t.start()
    me, core = lax.axis_index("tile"), lax.axis_index("chol")
    w, z = me // DEPTH, lax.rem(me, DEPTH)
    y, x = w // 4, lax.rem(w, 4)
    slabs, widths = (slab_a, slab_b, slab_c), (MAIN, MAIN, EDGE)
    rss, rbs, mines, inters = (rs_a, rs_b, rs_c), (rb_a, rb_b, rb_c), (mine_a, mine_b, mine_c), (inter_a, inter_b, inter_c)

    def plane(q):
        return lax.rem(y + q // 4, 4) * 4 + lax.rem(x + lax.rem(q, 4), 4)

    def level(d):
        return lax.rem(z + d + DEPTH, DEPTH)

    def near(dx, dy):
        return lax.rem(y + dy + 4, 4) * 4 + lax.rem(x + dx + 4, 4)

    def in_slab(column):
        return lax.rem(column, 2) * 8 + column // 2

    def remote(src, dst, send_sem, recv_sem, tile, to_core):
        return pltpu.make_async_remote_copy(src_ref=src, dst_ref=dst, send_sem=send_sem, recv_sem=recv_sem,
                                            device_id=(tile, to_core), device_id_type=MESH)

    def wait_bytes(ref, sem):
        pltpu.make_async_copy(ref, ref, sem).wait()

    def each(lo, hi, one):
        def step(q, _):
            one(q)
            return 0
        lax.fori_loop(lo, hi, step, 0)

    barrier = pltpu.get_barrier_semaphore()

    def greet(tile, to_core):
        pl.semaphore_signal(barrier, inc=1, device_id=(tile, to_core), device_id_type=MESH)

    @pl.when(core == 0)
    def _():
        each(1, COLS, lambda q: greet(plane(q) * DEPTH + z, 0))
        each(0, COLS, lambda q: greet(plane(q) * DEPTH + z, 1))
        each(1, DEPTH, lambda d: greet(w * DEPTH + level(d), 1))
        for d in (-1, 1):
            greet(w * DEPTH + level(d), 0)
        pl.semaphore_wait(barrier, 2 * COLS + DEPTH)

    @pl.when(core == 1)
    def _():
        each(0, DEPTH, lambda d: greet(w * DEPTH + level(d), 0))
        each(1, DEPTH, lambda d: greet(w * DEPTH + level(d), 1))
        each(1, COLS, lambda q: greet(plane(q) * DEPTH + z, 0))
        for dx, dy in ((1, 0), (-1, 0), (0, 1), (0, -1)):
            greet(near(dx, dy) * DEPTH + z, 1)
        pl.semaphore_wait(barrier, COLS + 2 * DEPTH + 2)

    low = lax.broadcasted_iota(jnp.int32, (16, 128), 1) < 64
    granule = lax.broadcasted_iota(jnp.int32, (16, 128), 1) // 8

    def halves(first, second):
        return (jnp.where(low, first, pltpu.roll(second, 64, 1)), jnp.where(low, pltpu.roll(first, 64, 1), second))

    def swap(blocks):
        for bit in (1, 2, 4):
            take = (granule & bit) != 0
            new = list(blocks)
            for i in range(8):
                if not i & bit:
                    first, second = blocks[i], blocks[i | bit]
                    new[i] = jnp.where(take, pltpu.roll(second, 8 * bit, 1), first)
                    new[i | bit] = jnp.where(take, second, pltpu.roll(first, 128 - 8 * bit, 1))
            blocks = new
        return blocks

    def tile_of(m):
        return pl.ds(pl.multiple_of(m * 128, 128), 128)

    def run(c):
        peers, blocks = PEERS[c], BLOCKS[c]
        wide = CUT * 8 * blocks

        def piece_of(buffer, n, place):
            if c == 0:
                return buffer.at[n, place // 2, :, pl.ds(pl.multiple_of(lax.rem(place, 2) * wide, 128), wide)]
            return buffer.at[n, place]

        own = z if c == 0 else in_slab(w)
        place_in_rows = w if c == 0 else z
        sent = []

        def peer(q):
            return plane(q) if c == 0 else level(q)

        def tile(q):
            return plane(q) * DEPTH + z if c == 0 else w * DEPTH + level(q)

        def vectors(owner, where, sem):
            if c != owner:
                return
            pltpu.make_async_copy(l_hbm.at[pl.ds(c * K, K), :, pl.ds(0, MAIN)], where.at[:, own], sem).start()
            theirs = in_slab(w) if c == 0 else z
            remote(l_hbm.at[pl.ds((1 - c) * K, K), :, pl.ds(0, MAIN)], where.at[:, theirs], swap_send.at[0], sem, me,
                   1 - c).start()

        def pass_on(p, rows, block, n, to):
            piece = slabs[p].at[rows, block]
            copy = remote(piece, piece, ring_send.at[n], ring_recv.at[n], to, c)
            copy.start()
            sent.append(copy)

        def z_ring(p, hop):
            for sub in range(4):
                for way in range(2):
                    if hop == 3 and sub % 2 != way:
                        continue
                    if hop:
                        z_arrived(p, sub, way, hop - 1)
                    pass_on(p, pl.ds(sub * 15, 15), level(-hop if way == 0 else hop), ((p * 4 + sub) * 2 + way) * 4 + hop,
                            w * DEPTH + level(1 if way == 0 else -1))

        def z_arrived(p, sub, way, hop):
            step = -1 - hop if way == 0 else 1 + hop
            wait_bytes(slabs[p].at[pl.ds(sub * 15, 15), level(step)], ring_recv.at[((p * 4 + sub) * 2 + way) * 4 + hop])

        def xy_number(p, half, a, b):
            return (p * 2 + half) * 16 + a % 4 * 4 + b % 4

        def xy_block(half, a, b):
            return in_slab(near(*((a, b) if half == 0 else (b, a))))

        def xy_send(p, half, second, way, a, b):
            to = near(way, 0) if (half == 0) != second else near(0, way)
            n = xy_number(p, half, a, b - way) if second else xy_number(p, half, a - way, b)
            pass_on(p, pl.ds(half * 30, 30), xy_block(half, a, b), n, to * DEPTH + z)

        def xy_arrived(p, half, a, b):
            wait_bytes(slabs[p].at[pl.ds(half * 30, 30), xy_block(half, a, b)], ring_recv.at[xy_number(p, half, a, b)])

        def xy_ring(p, stage):
            for half in range(2):
                if stage == 0:
                    for second in (False, True):
                        for way in (1, -1):
                            xy_send(p, half, second, way, 0, 0)
                if stage == 1:
                    for a in (3, 1):
                        xy_arrived(p, half, a, 0)
                        if a == 3:
                            xy_send(p, half, False, 1, a, 0)
                        for way in (1, -1):
                            xy_send(p, half, True, way, a, 0)
                if stage == 2:
                    xy_arrived(p, half, 0, 3)
                    xy_send(p, half, True, 1, 0, 3)
                    xy_arrived(p, half, 2, 0)
                    for way in (1, -1):
                        xy_send(p, half, True, way, 2, 0)
                if stage == 3:
                    for a in (3, 1):
                        xy_arrived(p, half, a, 1)
                        xy_send(p, half, True, -1, a, 1)
                    xy_arrived(p, half, 2, 3)
                    xy_send(p, half, True, 1, 2, 3)

        def last(p):
            if c == 0:
                for sub in range(4):
                    z_arrived(p, sub, 1 - sub % 2, 2)
                    z_arrived(p, sub, sub % 2, 3)
            else:
                for half in range(2):
                    for a, b in ((0, 1), (3, 3), (1, 3), (2, 1), (0, 2), (3, 2), (1, 2), (2, 2)):
                        xy_arrived(p, half, a, b)

        ring = z_ring if c == 0 else xy_ring

        def shuffle(n):
            if c == 0:
                def lane_tile(m):
                    for pair in range(CUT // 2):
                        k = n * CUT + 2 * pair
                        for side, block in enumerate(halves(t_ref[k, :, tile_of(m)],
                                                            t_ref[k + 1, :, tile_of(m)])):
                            at = side * wide + pair * 128
                            send[n, m, :, at:at + 128] = block
                each(0, COLS // 2, lane_tile)
            else:
                def one_row(k):
                    for i, block in enumerate(swap([t_ref[n * CUT + k, :, m * 128:(m + 1) * 128]
                                                    for m in range(8)])):
                        send[n, i, :, tile_of(k)] = block
                each(0, CUT, one_row)

        def unshuffle(n):
            if c == 0:
                def lane_tile(m):
                    for pair in range(CUT // 2):
                        lo, hi, k = pair * 128, wide + pair * 128, n * CUT + 2 * pair
                        for side, block in enumerate(halves(r_in[n, m, :, lo:lo + 128],
                                                            r_in[n, m, :, hi:hi + 128])):
                            out_ref[k + side, :, tile_of(m)] = block
                each(0, COLS // 2, lane_tile)
            else:
                def one_row(k):
                    for m, block in enumerate(swap([r_in[n, i, :, tile_of(k)] for i in range(8)])):
                        out_ref[n * CUT + k, :, m * 128:(m + 1) * 128] = block
                each(0, CUT, one_row)

        def exchange(n, into, send_sem, recv_sem):
            here = place_in_rows
            pltpu.make_async_copy(piece_of(send, n, here), piece_of(into, n, here), recv_sem.at[n]).start()
            each(1, peers, lambda q: remote(piece_of(send, n, peer(q)), piece_of(into, n, here), send_sem.at[n],
                                            recv_sem.at[n], tile(q), c).start())

        def all_but_one(n):
            if c == 0:
                return t_ref.at[pl.ds(0, COLS - 1), :, pl.ds(0, wide)]
            return t_in.at[n, pl.ds(0, DEPTH - 1)]

        def vectors_of(p, n):
            return slabs[p][n * CUT:(n + 1) * CUT, :blocks].reshape(wide, widths[p])

        def multiply1(p):
            total = None
            for n in range(CUTS):
                if c == 0:
                    rows = jnp.concatenate([t_in[n, :, :, :wide].reshape(128, wide), t_in[n, :, :, wide:].reshape(128, wide)])
                else:
                    rows = t_in[n].reshape(128, wide)
                term = jnp.dot(rows, vectors_of(p, n), preferred_element_type=F32)
                total = term if total is None else total + term
            rss[p][:peers] = total.astype(BF).reshape(peers, 2, 8, widths[p])

        def sums_of(place):
            return in_slab(place) if c == 0 else place

        def add_up(p):
            first = 0 if c == 0 else COLS
            pltpu.make_async_copy(rss[p].at[sums_of(place_in_rows), c], rbs[p].at[first], sum_recv.at[p]).start()

            def one(q):
                n, to_core = q // 2, lax.rem(q + c, 2)
                remote(rss[p].at[sums_of(peer(n)), to_core], rbs[p].at[first + n], sum_send.at[p], sum_recv.at[p], tile(n),
                       to_core).start()
            each(1, 2 * peers, one)

        def share(p):
            wait_bytes(rbs[p].at[pl.ds(0, SENDERS)], sum_recv.at[p])
            total = rbs[p][0].astype(F32)
            for n in range(1, SENDERS):
                total = total + rbs[p][n].astype(F32)
            mines[p][...] = total.astype(BF)
            pltpu.make_async_copy(mines[p], inters[p].at[place_in_rows, c], share_recv.at[p]).start()
            each(1 if c == 0 else 0, COLS, lambda q: remote(
                mines[p], inters[p].at[w, c], share_send.at[p], share_recv.at[p], plane(q) * DEPTH + z, 0).start())
            each(1 if c == 1 else 0, DEPTH, lambda d: remote(
                mines[p], inters[p].at[z, c], share_send.at[p], share_recv.at[p], w * DEPTH + level(d), 1).start())

        def multiply2(n):
            total = None
            for p in range(3):
                rows = inters[p][:peers].reshape(peers * 16, widths[p])
                term = lax.dot_general(rows, vectors_of(p, n), (((1,), (1,)), ((), ())), preferred_element_type=F32)
                total = term if total is None else total + term
            if c == 0:
                total = total.astype(BF).reshape(8, 2, 16, wide)
                send[n, :, :, :wide] = total[:, 0]
                send[n, :, :, wide:] = total[:, 1]
            else:
                send[n] = total.astype(BF).reshape(8, 16, wide)

        vectors(0, slab_a, own_sem.at[0])
        vectors(1, slab_b, own_sem.at[1])
        wait_bytes(slab_a.at[:, own], own_sem.at[0])
        ring(0, 0)
        load_l.wait()
        row = lax.broadcasted_iota(jnp.int32, (VEC - MAIN, EDGE), 0)
        column = lax.broadcasted_iota(jnp.int32, (VEC - MAIN, EDGE), 1)
        place = (column == row + (VEC - MAIN) * c).astype(BF)
        tail = jnp.dot(l_ref[:, :, MAIN:].reshape(2 * K * 8, VEC - MAIN), place, preferred_element_type=F32)
        edge[...] = tail.astype(BF).reshape(2 * K, 8, EDGE)
        to_sibling = remote(edge.at[pl.ds((1 - c) * K, K)], edge_in, edge_sem.at[0], edge_sem.at[1], me, 1 - c)
        to_sibling.start()
        load_t.wait()

        def deal(*cuts):
            for n in cuts:
                shuffle(n)
                exchange(n, t_in, t_send, t_recv)
        deal(0, 1, 2, 3)
        ring(0, 1)
        deal(4, 5, 6, 7)
        ring(0, 2)
        deal(8, 9)
        ring(0, 3)
        to_sibling.wait_recv()

        def merge(k):
            slab_c[k, own] = (edge[c * K + k].astype(F32) + edge_in[k].astype(F32)).astype(BF)
        each(0, K, merge)
        wait_bytes(slab_b.at[:, own], own_sem.at[1])
        ring(1, 0)
        ring(2, 0)
        ring(1, 1)
        ring(2, 1)
        last(0)
        for n in range(CUTS):
            wait_bytes(t_in.at[n], t_recv.at[n])
        multiply1(0)
        add_up(0)
        ring(1, 2)
        ring(2, 2)
        share(0)
        ring(1, 3)
        ring(2, 3)
        for n in range(CUTS):
            wait_bytes(all_but_one(n), t_send.at[n])
        last(1)
        multiply1(1)
        add_up(1)
        last(2)
        multiply1(2)
        add_up(2)
        share(1)
        share(2)
        for p in range(3):
            wait_bytes(inters[p].at[pl.ds(0, peers)], share_recv.at[p])
        for n in range(CUTS):
            multiply2(n)
            exchange(n, r_in, r_send, r_recv)
        for n in range(CUTS):
            wait_bytes(r_in.at[n], r_recv.at[n])
            unshuffle(n)

        for copy in sent + [to_sibling]:
            copy.wait_send()
        wait_bytes(slabs[c].at[:, own], swap_send.at[0])
        for n in range(CUTS):
            wait_bytes(all_but_one(n), r_send.at[n])
        for p in range(3):
            wait_bytes(rbs[p].at[pl.ds(0, 2 * peers - 1)], sum_send.at[p])
            wait_bytes(rbs[p].at[pl.ds(0, SENDERS - 1)], share_send.at[p])

    pl.when(core == 0)(lambda: run(0))
    pl.when(core == 1)(lambda: run(1))


def shards(amplitudes, cholesky):
    dma, V = pltpu.SemaphoreType.DMA, pltpu.VMEM
    widths = (MAIN, MAIN, EDGE)
    out = pl.pallas_call(
        kernel,
        out_shape=jax.ShapeDtypeStruct((K, 16, 1024), BF),
        in_specs=[pl.BlockSpec(memory_space=pl.ANY)] * 2,
        out_specs=pl.BlockSpec(memory_space=pltpu.VMEM),
        scratch_shapes=[
            V((K, 16, 1024), BF), V((2 * K, 8, VEC), BF),
            *[V((K, COLS, 8, n), BF) for n in widths],
            V((2 * K, 8, EDGE), BF), V((K, 8, EDGE), BF),
            *[V((CUTS, DEPTH, 16, CUT * 8 * COLS), BF)] * 3,
            *[V((COLS, 2, 8, n), BF) for n in widths], *[V((2 * COLS, 8, n), BF) for n in widths],
            *[V((8, n), BF) for n in widths], *[V((COLS, 2, 8, n), BF) for n in widths],
            dma((2,)), dma((1,)), dma((2,)), dma((96,)), dma((96,)), dma((CUTS,)), dma((CUTS,)),
            dma((3,)), dma((3,)), dma((3,)), dma((3,)), dma((CUTS,)), dma((CUTS,)), dma((2,)),
        ],
        compiler_params=pltpu.CompilerParams(has_side_effects=True, collective_id=0, vmem_limit_bytes=44 * 2**20),
    )(amplitudes.reshape(K, 16, 1024), cholesky)
    return out.reshape(amplitudes.shape)


def solution(mesh):
    in_specs = (P("chol", None, "tile", None), P(None, "tile", "chol"))
    out_specs = P("chol", None, "tile", None)
    return jax.shard_map(shards, mesh=mesh, in_specs=in_specs, out_specs=out_specs, check_vma=False)
```

```python
import jax
import jax.numpy as jnp
from jax import lax
from jax.experimental import pallas as pl
from jax.experimental.pallas import tpu as pltpu
from jax.sharding import PartitionSpec as P

MESH = pl.DeviceIdType.MESH
BF, F32 = jnp.bfloat16, jnp.float32
K, VEC = 60, 448
COLS, DEPTH = 16, 8
CUTS, CUT = 10, 6
SENDERS = COLS + DEPTH
MAIN, EDGE = 384, 128


PEERS, BLOCKS = (COLS, DEPTH), (DEPTH, COLS)


def kernel(t_hbm, l_hbm, out_ref, t_ref, l_ref, slab_a, slab_b, slab_c, edge, edge_in, send, t_in, r_in,
           rs_a, rs_b, rs_c, rb_a, rb_b, rb_c, mine_a, mine_b, mine_c, inter_a, inter_b, inter_c, own_sem, swap_send,
           edge_sem, ring_send, ring_recv, t_send, t_recv, sum_send, sum_recv, share_send, share_recv, r_send, r_recv,
           in_sem):
    load_l = pltpu.make_async_copy(l_hbm, l_ref, in_sem.at[0])
    load_l.start()
    load_t = pltpu.make_async_copy(t_hbm, t_ref, in_sem.at[1])
    load_t.start()
    me, core = lax.axis_index("tile"), lax.axis_index("chol")
    w, z = me // DEPTH, lax.rem(me, DEPTH)
    y, x = w // 4, lax.rem(w, 4)
    slabs, widths = (slab_a, slab_b, slab_c), (MAIN, MAIN, EDGE)
    rss, rbs, mines, inters = (rs_a, rs_b, rs_c), (rb_a, rb_b, rb_c), (mine_a, mine_b, mine_c), (inter_a, inter_b, inter_c)

    def plane(q):
        return lax.rem(y + q // 4, 4) * 4 + lax.rem(x + q % 4, 4)

    def level(d):
        return lax.rem(z + d + DEPTH, DEPTH)

    def near(dx, dy):
        return lax.rem(y + dy + 4, 4) * 4 + lax.rem(x + dx + 4, 4)

    def in_slab(column):
        return lax.rem(column, 2) * 8 + column // 2

    def remote(src, dst, send_sem, recv_sem, tile, to_core):
        return pltpu.make_async_remote_copy(src_ref=src, dst_ref=dst, send_sem=send_sem, recv_sem=recv_sem,
                                            device_id=(tile, to_core), device_id_type=MESH)

    def wait_bytes(ref, sem):
        pltpu.make_async_copy(ref, ref, sem).wait()

    def each(lo, hi, one):
        def step(q, _):
            one(q)
            return 0
        lax.fori_loop(lo, hi, step, 0)

    barrier = pltpu.get_barrier_semaphore()

    def greet(tile, to_core):
        pl.semaphore_signal(barrier, inc=1, device_id=(tile, to_core), device_id_type=MESH)

    @pl.when(core == 0)
    def _():
        each(1, COLS, lambda q: greet(plane(q) * DEPTH + z, 0))
        each(0, COLS, lambda q: greet(plane(q) * DEPTH + z, 1))
        each(1, DEPTH, lambda d: greet(w * DEPTH + level(d), 1))
        for d in (-1, 1):
            greet(w * DEPTH + level(d), 0)
        pl.semaphore_wait(barrier, 2 * COLS + DEPTH)

    @pl.when(core == 1)
    def _():
        each(0, DEPTH, lambda d: greet(w * DEPTH + level(d), 0))
        each(1, DEPTH, lambda d: greet(w * DEPTH + level(d), 1))
        each(1, COLS, lambda q: greet(plane(q) * DEPTH + z, 0))
        for dx, dy in ((1, 0), (-1, 0), (0, 1), (0, -1)):
            greet(near(dx, dy) * DEPTH + z, 1)
        pl.semaphore_wait(barrier, COLS + 2 * DEPTH + 2)

    low = lax.broadcasted_iota(jnp.int32, (16, 128), 1) < 64
    granule = lax.broadcasted_iota(jnp.int32, (16, 128), 1) // 8

    def halves(first, second):
        return (jnp.where(low, first, pltpu.roll(second, 64, 1)), jnp.where(low, pltpu.roll(first, 64, 1), second))

    def swap(blocks):
        for bit in (1, 2, 4):
            take = (granule & bit) != 0
            new = list(blocks)
            for i in range(8):
                if not i & bit:
                    first, second = blocks[i], blocks[i | bit]
                    new[i] = jnp.where(take, pltpu.roll(second, 8 * bit, 1), first)
                    new[i | bit] = jnp.where(take, second, pltpu.roll(first, 128 - 8 * bit, 1))
            blocks = new
        return blocks

    def tile_of(m):
        return pl.ds(pl.multiple_of(m * 128, 128), 128)

    def run(c):
        peers, blocks = PEERS[c], BLOCKS[c]
        wide = CUT * 8 * blocks

        def piece_of(buffer, n, place):
            if c == 0:
                return buffer.at[n, place // 2, :, pl.ds(pl.multiple_of(lax.rem(place, 2) * wide, 128), wide)]
            return buffer.at[n, place]

        own = z if c == 0 else in_slab(w)
        place_in_rows = w if c == 0 else z
        sent = []

        def peer(q):
            return plane(q) if c == 0 else level(q)

        def tile(q):
            return plane(q) * DEPTH + z if c == 0 else w * DEPTH + level(q)

        def vectors(owner, where, sem):
            if c != owner:
                return
            pltpu.make_async_copy(l_hbm.at[pl.ds(c * K, K), :, pl.ds(0, MAIN)], where.at[:, own], sem).start()
            theirs = in_slab(w) if c == 0 else z
            remote(l_hbm.at[pl.ds((1 - c) * K, K), :, pl.ds(0, MAIN)], where.at[:, theirs], swap_send.at[0], sem, me,
                   1 - c).start()

        def pass_on(p, rows, block, n, to):
            piece = slabs[p].at[rows, block]
            copy = remote(piece, piece, ring_send.at[n], ring_recv.at[n], to, c)
            copy.start()
            sent.append(copy)

        def z_ring(p, hop):
            for sub in range(4):
                for way in range(2):
                    if hop == 3 and sub % 2 != way:
                        continue
                    if hop:
                        z_arrived(p, sub, way, hop - 1)
                    pass_on(p, pl.ds(sub * 15, 15), level(-hop if way == 0 else hop), ((p * 4 + sub) * 2 + way) * 4 + hop,
                            w * DEPTH + level(1 if way == 0 else -1))

        def z_arrived(p, sub, way, hop):
            step = -1 - hop if way == 0 else 1 + hop
            wait_bytes(slabs[p].at[pl.ds(sub * 15, 15), level(step)], ring_recv.at[((p * 4 + sub) * 2 + way) * 4 + hop])

        def xy_number(p, half, a, b):
            return (p * 2 + half) * 16 + a % 4 * 4 + b % 4

        def xy_block(half, a, b):
            return in_slab(near(*((a, b) if half == 0 else (b, a))))

        def xy_send(p, half, second, way, a, b):
            to = near(way, 0) if (half == 0) != second else near(0, way)
            n = xy_number(p, half, a, b - way) if second else xy_number(p, half, a - way, b)
            pass_on(p, pl.ds(half * 30, 30), xy_block(half, a, b), n, to * DEPTH + z)

        def xy_arrived(p, half, a, b):
            wait_bytes(slabs[p].at[pl.ds(half * 30, 30), xy_block(half, a, b)], ring_recv.at[xy_number(p, half, a, b)])

        def xy_ring(p, stage):
            for half in range(2):
                if stage == 0:
                    for second in (False, True):
                        for way in (1, -1):
                            xy_send(p, half, second, way, 0, 0)
                if stage == 1:
                    for a in (3, 1):
                        xy_arrived(p, half, a, 0)
                        if a == 3:
                            xy_send(p, half, False, 1, a, 0)
                        for way in (1, -1):
                            xy_send(p, half, True, way, a, 0)
                if stage == 2:
                    xy_arrived(p, half, 0, 3)
                    xy_send(p, half, True, 1, 0, 3)
                    xy_arrived(p, half, 2, 0)
                    for way in (1, -1):
                        xy_send(p, half, True, way, 2, 0)
                if stage == 3:
                    for a in (3, 1):
                        xy_arrived(p, half, a, 1)
                        xy_send(p, half, True, -1, a, 1)
                    xy_arrived(p, half, 2, 3)
                    xy_send(p, half, True, 1, 2, 3)

        def last(p):
            if c == 0:
                for sub in range(4):
                    z_arrived(p, sub, 1 - sub % 2, 2)
                    z_arrived(p, sub, sub % 2, 3)
            else:
                for half in range(2):
                    for a, b in ((0, 1), (3, 3), (1, 3), (2, 1), (0, 2), (3, 2), (1, 2), (2, 2)):
                        xy_arrived(p, half, a, b)

        ring = z_ring if c == 0 else xy_ring

        def shuffle(n):
            if c == 0:
                def lane_tile(m):
                    for pair in range(CUT // 2):
                        k = n * CUT + 2 * pair
                        for side, block in enumerate(halves(t_ref[k, :, tile_of(m)],
                                                            t_ref[k + 1, :, tile_of(m)])):
                            at = side * wide + pair * 128
                            send[n, m, :, at:at + 128] = block
                each(0, COLS // 2, lane_tile)
            else:
                def one_row(k):
                    for i, block in enumerate(swap([t_ref[n * CUT + k, :, m * 128:(m + 1) * 128]
                                                    for m in range(8)])):
                        send[n, i, :, tile_of(k)] = block
                each(0, CUT, one_row)

        def unshuffle(n):
            if c == 0:
                def lane_tile(m):
                    for pair in range(CUT // 2):
                        lo, hi, k = pair * 128, wide + pair * 128, n * CUT + 2 * pair
                        for side, block in enumerate(halves(r_in[n, m, :, lo:lo + 128],
                                                            r_in[n, m, :, hi:hi + 128])):
                            out_ref[k + side, :, tile_of(m)] = block
                each(0, COLS // 2, lane_tile)
            else:
                def one_row(k):
                    for m, block in enumerate(swap([r_in[n, i, :, tile_of(k)] for i in range(8)])):
                        out_ref[n * CUT + k, :, m * 128:(m + 1) * 128] = block
                each(0, CUT, one_row)

        def exchange(n, into, send_sem, recv_sem):
            here = place_in_rows
            pltpu.make_async_copy(piece_of(send, n, here), piece_of(into, n, here), recv_sem.at[n]).start()
            each(1, peers, lambda q: remote(piece_of(send, n, peer(q)), piece_of(into, n, here), send_sem.at[n],
                                            recv_sem.at[n], tile(q), c).start())

        def all_but_one(n):
            if c == 0:
                return t_ref.at[pl.ds(0, COLS - 1), :, pl.ds(0, wide)]
            return t_in.at[n, pl.ds(0, DEPTH - 1)]

        def vectors_of(p, n):
            return slabs[p][n * CUT:(n + 1) * CUT, :blocks].reshape(wide, widths[p])

        def multiply1(p):
            total = None
            for n in range(CUTS):
                if c == 0:
                    rows = jnp.concatenate([t_in[n, :, :, :wide].reshape(128, wide), t_in[n, :, :, wide:].reshape(128, wide)])
                else:
                    rows = t_in[n].reshape(128, wide)
                term = jnp.dot(rows, vectors_of(p, n), preferred_element_type=F32)
                total = term if total is None else total + term
            rss[p][:peers] = total.astype(BF).reshape(peers, 2, 8, widths[p])

        def sums_of(place):
            return in_slab(place) if c == 0 else place

        def add_up(p):
            first = 0 if c == 0 else COLS
            pltpu.make_async_copy(rss[p].at[sums_of(place_in_rows), c], rbs[p].at[first], sum_recv.at[p]).start()

            def one(q):
                n, to_core = q // 2, (q + c) % 2
                remote(rss[p].at[sums_of(peer(n)), to_core], rbs[p].at[first + n], sum_send.at[p], sum_recv.at[p], tile(n),
                       to_core).start()
            for q in range(1, 2 * peers):
                one(q)

        def share(p):
            wait_bytes(rbs[p].at[pl.ds(0, SENDERS)], sum_recv.at[p])
            total = rbs[p][0].astype(F32)
            for n in range(1, SENDERS):
                total = total + rbs[p][n].astype(F32)
            mines[p][...] = total.astype(BF)
            pltpu.make_async_copy(mines[p], inters[p].at[place_in_rows, c], share_recv.at[p]).start()
            for q in range(1 if c == 0 else 0, COLS):
                remote(mines[p], inters[p].at[w, c], share_send.at[p], share_recv.at[p], plane(q) * DEPTH + z, 0).start()
            for d in range(1 if c == 1 else 0, DEPTH):
                remote(mines[p], inters[p].at[z, c], share_send.at[p], share_recv.at[p], w * DEPTH + level(d), 1).start()

        def multiply2(n):
            total = None
            for p in range(3):
                rows = inters[p][:peers].reshape(peers * 16, widths[p])
                term = lax.dot_general(rows, vectors_of(p, n), (((1,), (1,)), ((), ())), preferred_element_type=F32)
                total = term if total is None else total + term
            if c == 0:
                total = total.astype(BF).reshape(8, 2, 16, wide)
                send[n, :, :, :wide] = total[:, 0]
                send[n, :, :, wide:] = total[:, 1]
            else:
                send[n] = total.astype(BF).reshape(8, 16, wide)

        vectors(0, slab_a, own_sem.at[0])
        vectors(1, slab_b, own_sem.at[1])
        wait_bytes(slab_a.at[:, own], own_sem.at[0])
        ring(0, 0)
        load_l.wait()
        row = lax.broadcasted_iota(jnp.int32, (VEC - MAIN, EDGE), 0)
        column = lax.broadcasted_iota(jnp.int32, (VEC - MAIN, EDGE), 1)
        place = (column == row + (VEC - MAIN) * c).astype(BF)
        tail = jnp.dot(l_ref[:, :, MAIN:].reshape(2 * K * 8, VEC - MAIN), place, preferred_element_type=F32)
        edge[...] = tail.astype(BF).reshape(2 * K, 8, EDGE)
        to_sibling = remote(edge.at[pl.ds((1 - c) * K, K)], edge_in, edge_sem.at[0], edge_sem.at[1], me, 1 - c)
        to_sibling.start()
        load_t.wait()

        def deal(*cuts):
            for n in cuts:
                shuffle(n)
                exchange(n, t_in, t_send, t_recv)
        deal(0, 1, 2, 3)
        ring(0, 1)
        deal(4, 5, 6, 7)
        ring(0, 2)
        deal(8, 9)
        ring(0, 3)
        to_sibling.wait_recv()

        def merge(k):
            slab_c[k, own] = (edge[c * K + k].astype(F32) + edge_in[k].astype(F32)).astype(BF)
        each(0, K, merge)
        wait_bytes(slab_b.at[:, own], own_sem.at[1])
        ring(1, 0)
        ring(2, 0)
        ring(1, 1)
        ring(2, 1)
        last(0)
        for n in range(CUTS):
            wait_bytes(t_in.at[n], t_recv.at[n])
        multiply1(0)
        add_up(0)
        ring(1, 2)
        ring(2, 2)
        share(0)
        ring(1, 3)
        ring(2, 3)
        for n in range(CUTS):
            wait_bytes(all_but_one(n), t_send.at[n])
        last(1)
        multiply1(1)
        add_up(1)
        last(2)
        multiply1(2)
        add_up(2)
        share(1)
        share(2)
        for p in range(3):
            wait_bytes(inters[p].at[pl.ds(0, peers)], share_recv.at[p])
        for n in range(CUTS):
            multiply2(n)
            exchange(n, r_in, r_send, r_recv)
        for n in range(CUTS):
            wait_bytes(r_in.at[n], r_recv.at[n])
            unshuffle(n)

        for copy in sent + [to_sibling]:
            copy.wait_send()
        wait_bytes(slabs[c].at[:, own], swap_send.at[0])
        for n in range(CUTS):
            wait_bytes(all_but_one(n), r_send.at[n])
        for p in range(3):
            wait_bytes(rbs[p].at[pl.ds(0, 2 * peers - 1)], sum_send.at[p])
            wait_bytes(rbs[p].at[pl.ds(0, SENDERS - 1)], share_send.at[p])

    pl.when(core == 0)(lambda: run(0))
    pl.when(core == 1)(lambda: run(1))


def shards(amplitudes, cholesky):
    dma, V = pltpu.SemaphoreType.DMA, pltpu.VMEM
    widths = (MAIN, MAIN, EDGE)
    out = pl.pallas_call(
        kernel,
        out_shape=jax.ShapeDtypeStruct((K, 16, 1024), BF),
        in_specs=[pl.BlockSpec(memory_space=pl.ANY)] * 2,
        out_specs=pl.BlockSpec(memory_space=pltpu.VMEM),
        scratch_shapes=[
            V((K, 16, 1024), BF), V((2 * K, 8, VEC), BF),
            *[V((K, COLS, 8, n), BF) for n in widths],
            V((2 * K, 8, EDGE), BF), V((K, 8, EDGE), BF),
            *[V((CUTS, DEPTH, 16, CUT * 8 * COLS), BF)] * 3,
            *[V((COLS, 2, 8, n), BF) for n in widths], *[V((2 * COLS, 8, n), BF) for n in widths],
            *[V((8, n), BF) for n in widths], *[V((COLS, 2, 8, n), BF) for n in widths],
            dma((2,)), dma((1,)), dma((2,)), dma((96,)), dma((96,)), dma((CUTS,)), dma((CUTS,)),
            dma((3,)), dma((3,)), dma((3,)), dma((3,)), dma((CUTS,)), dma((CUTS,)), dma((2,)),
        ],
        compiler_params=pltpu.CompilerParams(has_side_effects=True, collective_id=0, vmem_limit_bytes=44 * 2**20),
    )(amplitudes.reshape(K, 16, 1024), cholesky)
    return out.reshape(amplitudes.shape)


def solution(mesh):
    in_specs = (P("chol", None, "tile", None), P(None, "tile", "chol"))
    out_specs = P("chol", None, "tile", None)
    return jax.shard_map(shards, mesh=mesh, in_specs=in_specs, out_specs=out_specs, check_vma=False)
```
